32 devices in a mesh: patch: 16 (over z, x, core), normal: 2 (over y).
Axes of the slice: x: 2, y: 2, z: 4, core: 2. Of those that a mesh axis runs over, the one named last changes fastest.
Arguments:
- residual_in: float32 [5, 128, 4096], P(None, 'normal', 'patch'), may hold values from -1.5 to 1.5
- prior_iterate: float32 [5, 128, 4096], P(None, 'normal', 'patch'), may hold values from -1.5 to 1.5
- coupling: float32 [4, 4096], P(None, 'patch'), may hold values from 0.2 to 0.6
- line_slot: int32 [4, 4096], P(None, 'patch'), may hold values from 0 to 127
- patch_nbr: int32 [16, 4], P('patch'), may hold values from 0 to 15, as said below
- edge_lines: int32 [16, 128], P('patch'), may hold values from 0 to 255, as said below
- upper_blocks: float32 [5, 5, 128, 4096], P(None, None, 'normal', 'patch'), may hold values from -1 to 1
- lower_blocks: float32 [5, 5, 128, 4096], P(None, None, 'normal', 'patch'), may hold values from -1 to 1
Outputs:
- adjoint: float32 [5, 128, 4096], P(None, 'normal', 'patch')
The draws below stay inside these ranges and needn't reach their ends.
Inputs may be any that keep to these rules, and one draw needn't show every extreme that they name: `patch_nbr`: each neighbour slot of patch p names a patch at cyclic distance 1 or 2 from p in patch order; slots may repeat. `edge_lines`: the 128 entries of a row are distinct.
All inputs are finite; a program needn't handle non-finite values.
Results may differ from the reference program's by a relative error of at most 0.0001.
Values sent between devices are 32-bit elements; how exact they have to be, the bound alone decides.
A program may use at most 64 MiB of HBM per device.

```python
import jax
import jax.numpy as jnp
from jax import lax

NV = 5
NB = 4
HALO = 128
LINES_DEV = 256
COLUMN_POINTS = 128
PATCHES = 16
COLUMN_COUNT = 4096


def draw_patch_nbr(key, part):
    key = jax.random.fold_in(key, 11)
    offsets = jnp.array([-2, -1, 1, 2], jnp.int32)
    chosen = jax.random.randint(key, (PATCHES, NB), 0, 4)
    shift_by = offsets[chosen]
    rows = jnp.arange(PATCHES, dtype=jnp.int32)[:, None]
    slots = jnp.arange(NB, dtype=jnp.int32)[None, :]
    forced = (rows <= 1) & (slots == 0)
    shift_by = jnp.where(forced, -1, shift_by)
    return ((rows + shift_by + 2 * PATCHES) % PATCHES).astype(jnp.int32)


def draw_edge_lines(key, part):
    key = jax.random.fold_in(key, 12)
    first_keys = jax.random.split(key, PATCHES)
    inner = jax.vmap(lambda single: jax.random.permutation(single, LINES_DEV - 2) + 1)(first_keys)
    inner = inner[:, :HALO - 2].astype(jnp.int32)
    ends = jnp.broadcast_to(jnp.array([0, LINES_DEV - 1], jnp.int32)[None, :], (PATCHES, 2))
    joined = jnp.concatenate([ends, inner], axis=1)
    second_keys = jax.random.split(jax.random.fold_in(key, 1), PATCHES)
    shuffle = jax.vmap(lambda single: jax.random.permutation(single, HALO))(second_keys)
    return jnp.take_along_axis(joined, shuffle.astype(jnp.int32), axis=1).astype(jnp.int32)


def line_rates(key, low_rate, high_rate):
    rate_key = jax.random.fold_in(key, 21)
    spread = jax.random.uniform(rate_key, (COLUMN_COUNT,), jnp.float32)
    return jnp.exp(jnp.log(low_rate) + spread * (jnp.log(high_rate) - jnp.log(low_rate)))


def reflect_blocks(key, damping_speeds):
    key_dir, position_seed, key_depth = jax.random.split(key, 3)
    direction = jax.random.normal(key_dir, (NV, COLUMN_POINTS, COLUMN_COUNT), jnp.float32)
    squares = jnp.sum(direction * direction, axis=0) + 0.01
    eye_part = jnp.eye(NV, dtype=jnp.float32)[:, :, None, None]
    mirror = eye_part - 2.0 * direction[:, None] * direction[None, :] / squares[None, None]
    spike_position = jax.random.uniform(position_seed, (COLUMN_POINTS, COLUMN_COUNT), jnp.float32)
    pass_extent = jax.random.uniform(key_depth, (COLUMN_POINTS, COLUMN_COUNT), jnp.float32, 0.5, 0.8)
    under_weighting = jnp.exp(-damping_speeds)[None, :] * jnp.where(spike_position < 3.0 / COLUMN_POINTS, pass_extent, 1.0)
    return mirror * under_weighting[None, None]


def draw_upper_blocks(key, part):
    damping_speeds = line_rates(key, 1.0 / (16.0 * COLUMN_POINTS), 1.0 / 30.0)
    key = jax.random.fold_in(key, 31)
    return reflect_blocks(key, damping_speeds)


def draw_lower_blocks(key, part):
    damping_speeds = line_rates(key, 1.0 / (16.0 * COLUMN_POINTS), 1.0 / 30.0)
    key = jax.random.fold_in(key, 32)
    return reflect_blocks(key, damping_speeds)


def plant(values, rng, least, high):
    longest = values.shape.index(max(values.shape))
    spots = []
    for shift in (0, 1):
        where = [jax.random.randint(jax.random.fold_in(rng, axis), (), 0, length) for axis, length in enumerate(values.shape)]
        where[longest] = (where[longest] + shift) % values.shape[longest]
        spots.append(tuple(where))
    return values.at[spots[0]].set(least).at[spots[1]].set(high)


def block_levels(rng, shape, pieces, smallest, high):
    def one(axis_at, shards_of):
        draws = jax.random.uniform(jax.random.fold_in(jax.random.fold_in(rng, 6), axis_at), (shards_of,), jnp.float32, smallest / len(pieces), high / len(pieces))
        return jnp.repeat(jnp.exp(draws), shape[axis_at] // shards_of).reshape((-1,) + (1,) * (len(shape) - axis_at - 1))

    gain = one(*pieces[0])
    for cut in pieces[1:]:
        gain = gain * one(*cut)
    return gain


def gaussian(stream_key, shape, scale, most, shards=(), kind=jnp.bfloat16):
    level = block_levels(stream_key, shape, shards, -0.22, 0.18) if shards else 1.0
    entries = jax.random.normal(stream_key, shape, jnp.float32) * scale * level
    return jnp.minimum(jnp.maximum(entries, -most), most).astype(kind)


def setup_inputs(seed: int = 0) -> dict:
    streams_of = jax.random.split(jax.random.key(seed), 9)
    return {
        "residual_in": gaussian(streams_of[0], (NV, COLUMN_POINTS, COLUMN_COUNT), 0.25, 1.5, ((1, 2), (2, 16)), jnp.float32),
        "prior_iterate": gaussian(streams_of[1], (NV, COLUMN_POINTS, COLUMN_COUNT), 0.25, 1.5, ((1, 2), (2, 16)), jnp.float32),
        "coupling": jnp.clip(0.2 + 0.400000021 * jax.random.uniform(streams_of[2], (NB, COLUMN_COUNT), jnp.float32) ** block_levels(streams_of[2], (NB, COLUMN_COUNT), ((1, 16),), -0.2, 0.2), 0.2, 0.6),
        "line_slot": plant(jax.random.randint(streams_of[3], (NB, COLUMN_COUNT), 0, HALO), jax.random.fold_in(streams_of[3], 1), 0, HALO - 1).astype(jnp.int32),
        "patch_nbr": draw_patch_nbr(jax.random.fold_in(streams_of[8], 71), 0),
        "edge_lines": draw_edge_lines(jax.random.fold_in(streams_of[8], 71), 0),
        "upper_blocks": draw_upper_blocks(jax.random.fold_in(streams_of[8], 71), 0),
        "lower_blocks": draw_lower_blocks(jax.random.fold_in(streams_of[8], 71), 0),
    }


HIGHEST = lax.Precision.HIGHEST


def line_sweep(blocks, forcing, reverse):
    def advance(state_now, inputs):
        block_here, force_here = inputs
        new_state = force_here - jnp.einsum("wvl,wl->vl", block_here, state_now, precision=HIGHEST)
        return new_state, new_state

    start_state = jnp.zeros((forcing.shape[0], forcing.shape[2]), jnp.float32)
    inputs = (jnp.moveaxis(blocks, 2, 0), jnp.moveaxis(forcing, 1, 0))
    _, states = lax.scan(advance, start_state, inputs, reverse=reverse)
    return jnp.moveaxis(states, 0, 1)


def reference(residual_in, prior_iterate, coupling, line_slot, patch_nbr, edge_lines, upper_blocks, lower_blocks):
    grouped = prior_iterate.reshape(NV, COLUMN_POINTS, PATCHES, LINES_DEV)
    strips = jnp.take_along_axis(grouped, edge_lines[None, None, :, :], axis=3)
    slots_by_patch = jnp.moveaxis(line_slot.reshape(NB, PATCHES, LINES_DEV), 1, 0)
    weights_by_patch = jnp.moveaxis(coupling.reshape(NB, PATCHES, LINES_DEV), 1, 0)

    def offline_patch(inputs):
        nbr_row, slot_rows, weight_rows = inputs
        source = jnp.moveaxis(strips[:, :, nbr_row, :], 2, 0)
        picked = jnp.take_along_axis(source, slot_rows[:, None, None, :], axis=3)
        return jnp.sum(picked * weight_rows[:, None, None, :], axis=0)

    offline = lax.map(offline_patch, (patch_nbr, slots_by_patch, weights_by_patch))
    offline = jnp.moveaxis(offline, 0, 2).reshape(NV, COLUMN_POINTS, COLUMN_COUNT)
    forcing = residual_in - offline
    upward = line_sweep(upper_blocks, forcing, False)
    return line_sweep(lower_blocks, upward, True)
```

```python
import functools

import jax
import jax.numpy as jnp
from jax import lax
from jax.experimental import pallas as pl
from jax.experimental.pallas import tpu as pltpu
from jax.sharding import PartitionSpec as P

MESH = pl.DeviceIdType.MESH
CHUNK = 8
LANES = 128
F32 = jnp.float32
BF16 = jnp.bfloat16


def halves(x):
    high = x.astype(BF16)
    return high, (x - high.astype(F32)).astype(BF16)


def dot(a, b):
    return jnp.dot(a, b, preferred_element_type=F32)


def kernel(
    patches,
    count,
    prior_ref,
    coupling_ref,
    slot_ref,
    nbr_ref,
    edge_ref,
    residual_hbm,
    upper_hbm,
    lower_hbm,
    out_ref,
    residual,
    upper,
    lower,
    strip,
    halo,
    weight_hi,
    weight_lo,
    maps,
    force,
    up_state,
    up_out,
    up_in,
    down_out,
    down_in,
    local_sem,
    strip_send,
    strip_recv,
    line_send,
    line_recv,
):
    nv, cells, lines = prior_ref.shape
    slots = coupling_ref.shape[0]
    width = edge_ref.shape[1]
    seg = cells // CHUNK
    own = lax.axis_index("patch")
    place = lax.axis_index("normal")

    tiles = lines // LANES
    loads = [pltpu.make_async_copy(residual_hbm, residual, local_sem.at[2, 0])]
    for i, (src, dst) in enumerate(((upper_hbm, upper), (lower_hbm, lower))):
        for t in range(tiles):
            part = src.at[:, :, :, t * LANES : (t + 1) * LANES]
            loads.append(pltpu.make_async_copy(part, dst.at[t], local_sem.at[i, t]))
    for load in loads:
        load.start()

    core = lax.rem(own, 2)
    chip = lax.rem(own // 2, 2)
    core_mate = own + 1 - 2 * core
    chip_mate = own + 2 - 4 * chip
    ahead = lax.rem(own + 4 - 8 * chip + patches, patches)
    behind = lax.rem(own - 4 + 8 * chip + patches, patches)
    direct = 3 - 3 * chip

    barrier = pltpu.get_barrier_semaphore()
    for other in (core_mate, chip_mate, behind):
        pl.semaphore_signal(barrier, inc=1, device_id={"patch": other}, device_id_type=MESH)

    @pl.when(place > 0)
    def _():
        pl.semaphore_signal(barrier, inc=1, device_id={"normal": place - 1}, device_id_type=MESH)

    @pl.when(place < count - 1)
    def _():
        pl.semaphore_signal(barrier, inc=1, device_id={"normal": place + 1}, device_id_type=MESH)

    pick = jnp.where(
        lax.broadcasted_iota(jnp.int32, (lines, width), 0) == edge_ref[...], 1.0, 0.0
    ).astype(BF16)
    prior = prior_ref[...].reshape(nv * cells, lines)
    high = prior.astype(BF16)
    rest = prior - high.astype(F32)
    middle, low = halves(rest)
    exported = dot(high, pick) + (dot(middle, pick) + dot(low, pick))
    strip[...] = exported.reshape(nv, cells, width)

    below = (place + count - 1) // count
    above = (2 * count - 2 - place) // count
    pl.semaphore_wait(barrier, 3 + below + above)

    def send(kind, v, src, slot, other):
        return pltpu.make_async_remote_copy(
            src_ref=src,
            dst_ref=halo.at[slot, v],
            send_sem=strip_send.at[kind, v],
            recv_sem=strip_recv.at[kind, v],
            device_id={"patch": other},
            device_id_type=MESH,
        )

    to_chip = [send(0, v, strip.at[v], 3 - direct, chip_mate) for v in range(nv)]
    to_core = [send(1, v, strip.at[v], 1 + core, core_mate) for v in range(nv)]
    onward = [send(2, v, halo.at[direct, v], 3 - direct, ahead) for v in range(nv)]
    across = [send(3, v, halo.at[3 - 3 * core, v], 2 - core, core_mate) for v in range(nv)]
    for copy in to_chip + to_core:
        copy.start()

    row = lax.broadcasted_iota(jnp.int32, (width, lines), 0)
    offsets = (patches - 2, patches - 1, 1, 2)
    for s in range(4):
        total = jnp.zeros((width, lines), F32)
        for k in range(slots):
            relative = lax.rem(nbr_ref[0, k] - own + patches, patches)
            key = jnp.where(relative == offsets[s], slot_ref[k : k + 1, :], -1)
            total = total + jnp.where(row == key, coupling_ref[k : k + 1, :], 0.0)
        whi, wlo = halves(total)
        weight_hi[s * width : (s + 1) * width, :] = whi
        weight_lo[s * width : (s + 1) * width, :] = wlo

    def spread(ref, j, *at):
        parts = [ref[(t, *at, pl.ds(j, CHUNK, stride=seg))] for t in range(tiles)]
        return jnp.concatenate(parts, axis=1)

    def block(ref, w, v, j):
        return spread(ref, j, w, v)

    def advance(ref, j, state):
        result = []
        for v in range(nv):
            terms = [block(ref, w, v, j) * state[w] for w in range(nv)]
            result.append(((terms[0] + terms[1]) + (terms[2] + terms[3])) + terms[4])
        return result

    chunk_row = lax.broadcasted_iota(jnp.int32, (CHUNK, lines), 0)

    def shifted(x, by, reverse, fill):
        if reverse:
            return jnp.where(chunk_row < CHUNK - by, pltpu.roll(x, CHUNK - by, 0), fill)
        return jnp.where(chunk_row >= by, pltpu.roll(x, by, 0), fill)

    def map_column(ref, which, column, reverse):
        start = tuple(
            jnp.full((CHUNK, lines), 1.0 if v == column else 0.0, F32) for v in range(nv)
        )

        def one(step, state):
            j = seg - 1 - step if reverse else step
            return tuple(-x for x in advance(ref, j, state))

        end = lax.fori_loop(0, seg, one, start)
        for v in range(nv):
            maps[which, 0, v, column] = end[v]

    for load in loads:
        load.wait()
    for v in range(nv):
        to_chip[v].wait_recv()
        onward[v].start()
        map_column(upper, 0, v, False)
        map_column(lower, 1, v, True)

    def join(which, level, reverse):
        by = 1 << level
        for column in range(nv):
            prev = [
                shifted(maps[which, level, w, column], by, reverse, 1.0 if w == column else 0.0)
                for w in range(nv)
            ]
            for v in range(nv):
                total = maps[which, level, v, 0] * prev[0]
                for w in range(1, nv):
                    total = total + maps[which, level, v, w] * prev[w]
                maps[which, level + 1, v, column] = total

    for v in range(nv):
        onward[v].wait_recv()
        across[v].start()
        if v < 3:
            join(0, v, False)
            join(1, v, True)

    for v in range(nv):
        to_core[v].wait_recv()
        across[v].wait_recv()
    source = jnp.concatenate([halo[s].reshape(nv * cells, width) for s in range(4)], axis=1)
    source_hi, source_lo = halves(source)
    whole_hi = weight_hi[...]
    offline = dot(source_hi, whole_hi) + (dot(source_lo, whole_hi) + dot(source_hi, weight_lo[...]))
    forcing = residual[...] - offline.reshape(nv, cells, lines)
    for t in range(tiles):
        force[t] = forcing[:, :, t * LANES : (t + 1) * LANES]

    def read_force(v, j):
        return spread(force, j, v)

    def read_up(v, j):
        return up_state[v, j]

    def store_up(v, j, value):
        up_state[v, j] = value

    def store_out(v, j, value):
        for t in range(tiles):
            part = value[:, t * LANES : (t + 1) * LANES]
            force[t, v, pl.ds(j, CHUNK, stride=seg), :] = part

    def sweep(ref, which, reverse, read, store, sender, receiver, out_buf, in_buf):
        order = range(seg - 1, -1, -1) if reverse else range(seg)
        state = None
        for j in order:
            rhs = [read(v, j) for v in range(nv)]
            if state is None:
                state = rhs
            else:
                step = advance(ref, j, state)
                state = [a - b for a, b in zip(rhs, step)]
        for level in range(3):
            prev = [shifted(x, 1 << level, reverse, 0.0) for x in state]
            fresh = []
            for v in range(nv):
                terms = [maps[which, level, v, w] * prev[w] for w in range(nv)]
                fresh.append(
                    state[v] + (((terms[0] + terms[1]) + (terms[2] + terms[3])) + terms[4])
                )
            state = fresh

        has_source = place < count - 1 if reverse else place > 0
        has_target = place > 0 if reverse else place < count - 1

        @pl.when(has_source)
        def _():
            receiver.wait_recv()

        carried = [jnp.where(has_source, in_buf[v : v + 1, :], 0.0) for v in range(nv)]
        full = []
        for v in range(nv):
            terms = [maps[which, 3, v, w] * carried[w] for w in range(nv)]
            full.append(state[v] + (((terms[0] + terms[1]) + (terms[2] + terms[3])) + terms[4]))
        end = 0 if reverse else CHUNK - 1
        for v in range(nv):
            out_buf[v : v + 1, :] = full[v][end : end + 1, :]

        @pl.when(has_target)
        def _():
            sender.start()

        now = [shifted(full[v], 1, reverse, carried[v]) for v in range(nv)]
        for j in order:
            step = advance(ref, j, now)
            now = [read(v, j) - step[v] for v in range(nv)]
            for v in range(nv):
                store(v, j, now[v])

    def carry(kind, src, dst, other):
        return pltpu.make_async_remote_copy(
            src_ref=src,
            dst_ref=dst,
            send_sem=line_send.at[kind],
            recv_sem=line_recv.at[kind],
            device_id={"normal": other},
            device_id_type=MESH,
        )

    go_up = carry(0, up_out, up_in, place + 1)
    go_down = carry(1, down_out, down_in, place - 1)
    up_out[...] = jnp.zeros_like(up_out)
    down_out[...] = jnp.zeros_like(down_out)
    sweep(upper, 0, False, read_force, store_up, go_up, go_up, up_out, up_in)
    sweep(lower, 1, True, read_up, store_out, go_down, go_down, down_out, down_in)

    for t in range(tiles):
        out_ref[:, :, t * LANES : (t + 1) * LANES] = force[t]

    for copy in to_chip + to_core + onward + across:
        copy.wait_send()

    @pl.when(place < count - 1)
    def _():
        go_up.wait_send()

    @pl.when(place > 0)
    def _():
        go_down.wait_send()


def local(
    patches,
    count,
    residual_in,
    prior_iterate,
    coupling,
    line_slot,
    patch_nbr,
    edge_lines,
    upper_blocks,
    lower_blocks,
):
    nv, cells, lines = residual_in.shape
    width = edge_lines.shape[1]
    vmem = pl.BlockSpec(memory_space=pltpu.VMEM)
    hbm = pl.BlockSpec(memory_space=pl.ANY)
    seg = cells // CHUNK
    tiles = lines // LANES
    return pl.pallas_call(
        functools.partial(kernel, patches, count),
        out_shape=jax.ShapeDtypeStruct(residual_in.shape, F32),
        in_specs=[
            vmem,
            vmem,
            vmem,
            pl.BlockSpec(memory_space=pltpu.SMEM),
            vmem,
            hbm,
            hbm,
            hbm,
        ],
        out_specs=vmem,
        scratch_shapes=[
            pltpu.VMEM(residual_in.shape, F32),
            pltpu.VMEM((tiles, nv, nv, cells, LANES), F32),
            pltpu.VMEM((tiles, nv, nv, cells, LANES), F32),
            pltpu.VMEM((nv, cells, width), F32),
            pltpu.VMEM((4, nv, cells, width), F32),
            pltpu.VMEM((4 * width, lines), BF16),
            pltpu.VMEM((4 * width, lines), BF16),
            pltpu.VMEM((2, 4, nv, nv, CHUNK, lines), F32),
            pltpu.VMEM((tiles, nv, cells, LANES), F32),
            pltpu.VMEM((nv, seg, CHUNK, lines), F32),
            pltpu.VMEM((8, lines), F32),
            pltpu.VMEM((8, lines), F32),
            pltpu.VMEM((8, lines), F32),
            pltpu.VMEM((8, lines), F32),
            pltpu.SemaphoreType.DMA((3, tiles)),
            pltpu.SemaphoreType.DMA((4, nv)),
            pltpu.SemaphoreType.DMA((4, nv)),
            pltpu.SemaphoreType.DMA((2,)),
            pltpu.SemaphoreType.DMA((2,)),
        ],
        compiler_params=pltpu.CompilerParams(
            collective_id=0, has_side_effects=True, vmem_limit_bytes=40 * 2**20
        ),
    )(
        prior_iterate,
        coupling,
        line_slot,
        patch_nbr,
        edge_lines,
        residual_in,
        upper_blocks,
        lower_blocks,
    )


def solution(mesh):
    in_specs = (
        P(None, "normal", "patch"),
        P(None, "normal", "patch"),
        P(None, "patch"),
        P(None, "patch"),
        P("patch", None),
        P("patch", None),
        P(None, None, "normal", "patch"),
        P(None, None, "normal", "patch"),
    )
    body = functools.partial(local, mesh.shape["patch"], mesh.shape["normal"])
    return jax.shard_map(
        body, mesh=mesh, in_specs=in_specs, out_specs=P(None, "normal", "patch"), check_vma=False
    )
```

```python
import functools

import jax
import jax.numpy as jnp
from jax import lax
from jax.experimental import pallas as pl
from jax.experimental.pallas import tpu as pltpu
from jax.sharding import PartitionSpec as P

MESH = pl.DeviceIdType.MESH
CHUNK = 8
LANES = 128
F32 = jnp.float32
BF16 = jnp.bfloat16


def halves(x):
    high = x.astype(BF16)
    return high, (x - high.astype(F32)).astype(BF16)


def dot(a, b):
    return jnp.dot(a, b, preferred_element_type=F32)


def kernel(
    patches,
    count,
    prior_hbm,
    coupling_hbm,
    slot_hbm,
    nbr_ref,
    edge_hbm,
    residual_hbm,
    upper_hbm,
    lower_hbm,
    out_ref,
    prior_ref,
    coupling_ref,
    slot_ref,
    edge_ref,
    residual,
    upper,
    lower,
    strip,
    halo,
    weight_hi,
    weight_lo,
    maps,
    force,
    up_state,
    up_out,
    up_in,
    down_out,
    down_in,
    local_sem,
    first_sem,
    strip_send,
    strip_recv,
    line_send,
    line_recv,
):
    nv, cells, lines = prior_ref.shape
    slots = coupling_ref.shape[0]
    width = edge_ref.shape[1]
    seg = cells // CHUNK
    own = lax.axis_index("patch")
    place = lax.axis_index("normal")

    first = [
        pltpu.make_async_copy(src, dst, first_sem.at[i])
        for i, (src, dst) in enumerate(
            (
                (edge_hbm, edge_ref),
                (prior_hbm, prior_ref),
                (coupling_hbm, coupling_ref),
                (slot_hbm, slot_ref),
            )
        )
    ]
    for load in first:
        load.start()
    tiles = lines // LANES
    loads = [pltpu.make_async_copy(residual_hbm, residual, local_sem.at[2, 0])]
    for i, (src, dst) in enumerate(((upper_hbm, upper), (lower_hbm, lower))):
        for t in range(tiles):
            part = src.at[:, :, :, t * LANES : (t + 1) * LANES]
            loads.append(pltpu.make_async_copy(part, dst.at[t], local_sem.at[i, t]))
    for load in loads:
        load.start()

    core = lax.rem(own, 2)
    chip = lax.rem(own // 2, 2)
    core_mate = own + 1 - 2 * core
    chip_mate = own + 2 - 4 * chip
    corner = lax.rem(chip_mate - 4 + 8 * chip + patches, patches)
    source_corner = lax.rem(own - 4 + 8 * chip + patches, patches) + 2 - 4 * chip
    direct = 3 - 3 * chip

    barrier = pltpu.get_barrier_semaphore()
    for other in (core_mate, chip_mate, source_corner):
        pl.semaphore_signal(barrier, inc=1, device_id={"patch": other}, device_id_type=MESH)

    @pl.when(place > 0)
    def _():
        pl.semaphore_signal(barrier, inc=1, device_id={"normal": place - 1}, device_id_type=MESH)

    @pl.when(place < count - 1)
    def _():
        pl.semaphore_signal(barrier, inc=1, device_id={"normal": place + 1}, device_id_type=MESH)

    for load in first:
        load.wait()
    pick = jnp.where(
        lax.broadcasted_iota(jnp.int32, (lines, width), 0) == edge_ref[...], 1.0, 0.0
    ).astype(BF16)
    prior = prior_ref[...].reshape(nv * cells, lines)
    high = prior.astype(BF16)
    rest = prior - high.astype(F32)
    middle, low = halves(rest)
    exported = dot(high, pick) + (dot(middle, pick) + dot(low, pick))
    strip[...] = exported.reshape(nv, cells, width)

    below = (place + count - 1) // count
    above = (2 * count - 2 - place) // count
    pl.semaphore_wait(barrier, 3 + below + above)

    def send(kind, v, src, slot, other):
        return pltpu.make_async_remote_copy(
            src_ref=src,
            dst_ref=halo.at[slot, v],
            send_sem=strip_send.at[kind, v],
            recv_sem=strip_recv.at[kind, v],
            device_id={"patch": other},
            device_id_type=MESH,
        )

    to_chip = [send(0, v, strip.at[v], 3 - direct, chip_mate) for v in range(nv)]
    to_core = [send(1, v, strip.at[v], 1 + core, core_mate) for v in range(nv)]
    onward = [send(2, v, strip.at[v], direct, corner) for v in range(nv)]
    across = [send(3, v, halo.at[3 - 3 * core, v], 2 - core, core_mate) for v in range(nv)]
    for copy in to_chip + onward + to_core:
        copy.start()

    row = lax.broadcasted_iota(jnp.int32, (width, lines), 0)
    offsets = (patches - 2, patches - 1, 1, 2)
    for s in range(4):
        total = jnp.zeros((width, lines), F32)
        for k in range(slots):
            relative = lax.rem(nbr_ref[0, k] - own + patches, patches)
            key = jnp.where(relative == offsets[s], slot_ref[k : k + 1, :], -1)
            total = total + jnp.where(row == key, coupling_ref[k : k + 1, :], 0.0)
        whi, wlo = halves(total)
        weight_hi[s * width : (s + 1) * width, :] = whi
        weight_lo[s * width : (s + 1) * width, :] = wlo

    def spread(ref, j, *at):
        parts = [ref[(t, *at, pl.ds(j, CHUNK, stride=seg))] for t in range(tiles)]
        return jnp.concatenate(parts, axis=1)

    def block(ref, w, v, j):
        return spread(ref, j, w, v)

    def advance(ref, j, state):
        result = []
        for v in range(nv):
            terms = [block(ref, w, v, j) * state[w] for w in range(nv)]
            result.append(((terms[0] + terms[1]) + (terms[2] + terms[3])) + terms[4])
        return result

    chunk_row = lax.broadcasted_iota(jnp.int32, (CHUNK, lines), 0)

    def shifted(x, by, reverse, fill):
        if reverse:
            return jnp.where(chunk_row < CHUNK - by, pltpu.roll(x, CHUNK - by, 0), fill)
        return jnp.where(chunk_row >= by, pltpu.roll(x, by, 0), fill)

    def map_column(ref, which, column, reverse):
        start = tuple(
            jnp.full((CHUNK, lines), 1.0 if v == column else 0.0, F32) for v in range(nv)
        )

        def one(step, state):
            j = seg - 1 - step if reverse else step
            return tuple(-x for x in advance(ref, j, state))

        end = lax.fori_loop(0, seg, one, start)
        for v in range(nv):
            maps[which, 0, v, column] = end[v]

    for load in loads:
        load.wait()
    for v in range(nv):
        to_chip[v].wait_recv()
        map_column(upper, 0, v, False)
        map_column(lower, 1, v, True)

    def join(which, level, reverse):
        by = 1 << level
        for column in range(nv):
            prev = [
                shifted(maps[which, level, w, column], by, reverse, 1.0 if w == column else 0.0)
                for w in range(nv)
            ]
            for v in range(nv):
                total = maps[which, level, v, 0] * prev[0]
                for w in range(1, nv):
                    total = total + maps[which, level, v, w] * prev[w]
                maps[which, level + 1, v, column] = total

    for v in range(nv):
        onward[v].wait_recv()
        across[v].start()
        if v < 3:
            join(0, v, False)
            join(1, v, True)

    for v in range(nv):
        to_core[v].wait_recv()
        across[v].wait_recv()
    source = jnp.concatenate([halo[s].reshape(nv * cells, width) for s in range(4)], axis=1)
    source_hi, source_lo = halves(source)
    whole_hi = weight_hi[...]
    offline = dot(source_hi, whole_hi) + (dot(source_lo, whole_hi) + dot(source_hi, weight_lo[...]))
    forcing = residual[...] - offline.reshape(nv, cells, lines)
    for t in range(tiles):
        force[t] = forcing[:, :, t * LANES : (t + 1) * LANES]

    def read_force(v, j):
        return spread(force, j, v)

    def read_up(v, j):
        return up_state[v, j]

    def store_up(v, j, value):
        up_state[v, j] = value

    def store_out(v, j, value):
        for t in range(tiles):
            part = value[:, t * LANES : (t + 1) * LANES]
            force[t, v, pl.ds(j, CHUNK, stride=seg), :] = part

    def sweep(ref, which, reverse, read, store, sender, receiver, out_buf, in_buf):
        order = range(seg - 1, -1, -1) if reverse else range(seg)
        state = None
        for j in order:
            rhs = [read(v, j) for v in range(nv)]
            if state is None:
                state = rhs
            else:
                step = advance(ref, j, state)
                state = [a - b for a, b in zip(rhs, step)]
        for level in range(3):
            prev = [shifted(x, 1 << level, reverse, 0.0) for x in state]
            fresh = []
            for v in range(nv):
                terms = [maps[which, level, v, w] * prev[w] for w in range(nv)]
                fresh.append(
                    state[v] + (((terms[0] + terms[1]) + (terms[2] + terms[3])) + terms[4])
                )
            state = fresh

        has_source = place < count - 1 if reverse else place > 0
        has_target = place > 0 if reverse else place < count - 1

        @pl.when(has_source)
        def _():
            receiver.wait_recv()

        carried = [jnp.where(has_source, in_buf[v : v + 1, :], 0.0) for v in range(nv)]
        full = []
        for v in range(nv):
            terms = [maps[which, 3, v, w] * carried[w] for w in range(nv)]
            full.append(state[v] + (((terms[0] + terms[1]) + (terms[2] + terms[3])) + terms[4]))
        end = 0 if reverse else CHUNK - 1
        for v in range(nv):
            out_buf[v : v + 1, :] = full[v][end : end + 1, :]

        @pl.when(has_target)
        def _():
            sender.start()

        now = [shifted(full[v], 1, reverse, carried[v]) for v in range(nv)]
        for j in order:
            step = advance(ref, j, now)
            now = [read(v, j) - step[v] for v in range(nv)]
            for v in range(nv):
                store(v, j, now[v])

    def carry(kind, src, dst, other):
        return pltpu.make_async_remote_copy(
            src_ref=src,
            dst_ref=dst,
            send_sem=line_send.at[kind],
            recv_sem=line_recv.at[kind],
            device_id={"normal": other},
            device_id_type=MESH,
        )

    go_up = carry(0, up_out, up_in, place + 1)
    go_down = carry(1, down_out, down_in, place - 1)
    up_out[...] = jnp.zeros_like(up_out)
    down_out[...] = jnp.zeros_like(down_out)
    sweep(upper, 0, False, read_force, store_up, go_up, go_up, up_out, up_in)
    sweep(lower, 1, True, read_up, store_out, go_down, go_down, down_out, down_in)

    for t in range(tiles):
        out_ref[:, :, t * LANES : (t + 1) * LANES] = force[t]

    for copy in to_chip + to_core + onward + across:
        copy.wait_send()

    @pl.when(place < count - 1)
    def _():
        go_up.wait_send()

    @pl.when(place > 0)
    def _():
        go_down.wait_send()


def local(
    patches,
    count,
    residual_in,
    prior_iterate,
    coupling,
    line_slot,
    patch_nbr,
    edge_lines,
    upper_blocks,
    lower_blocks,
):
    nv, cells, lines = residual_in.shape
    width = edge_lines.shape[1]
    vmem = pl.BlockSpec(memory_space=pltpu.VMEM)
    hbm = pl.BlockSpec(memory_space=pltpu.HBM)
    seg = cells // CHUNK
    tiles = lines // LANES
    return pl.pallas_call(
        functools.partial(kernel, patches, count),
        out_shape=jax.ShapeDtypeStruct(residual_in.shape, F32),
        in_specs=[
            hbm,
            hbm,
            hbm,
            pl.BlockSpec(memory_space=pltpu.SMEM),
            hbm,
            hbm,
            hbm,
            hbm,
        ],
        out_specs=vmem,
        scratch_shapes=[
            pltpu.VMEM(prior_iterate.shape, F32),
            pltpu.VMEM(coupling.shape, F32),
            pltpu.VMEM(line_slot.shape, jnp.int32),
            pltpu.VMEM(edge_lines.shape, jnp.int32),
            pltpu.VMEM(residual_in.shape, F32),
            pltpu.VMEM((tiles, nv, nv, cells, LANES), F32),
            pltpu.VMEM((tiles, nv, nv, cells, LANES), F32),
            pltpu.VMEM((nv, cells, width), F32),
            pltpu.VMEM((4, nv, cells, width), F32),
            pltpu.VMEM((4 * width, lines), BF16),
            pltpu.VMEM((4 * width, lines), BF16),
            pltpu.VMEM((2, 4, nv, nv, CHUNK, lines), F32),
            pltpu.VMEM((tiles, nv, cells, LANES), F32),
            pltpu.VMEM((nv, seg, CHUNK, lines), F32),
            pltpu.VMEM((8, lines), F32),
            pltpu.VMEM((8, lines), F32),
            pltpu.VMEM((8, lines), F32),
            pltpu.VMEM((8, lines), F32),
            pltpu.SemaphoreType.DMA((3, tiles)),
            pltpu.SemaphoreType.DMA((4,)),
            pltpu.SemaphoreType.DMA((4, nv)),
            pltpu.SemaphoreType.DMA((4, nv)),
            pltpu.SemaphoreType.DMA((2,)),
            pltpu.SemaphoreType.DMA((2,)),
        ],
        compiler_params=pltpu.CompilerParams(
            collective_id=0, has_side_effects=True, vmem_limit_bytes=60 * 2**20
        ),
    )(
        prior_iterate,
        coupling,
        line_slot,
        patch_nbr,
        edge_lines,
        residual_in,
        upper_blocks,
        lower_blocks,
    )


def solution(mesh):
    in_specs = (
        P(None, "normal", "patch"),
        P(None, "normal", "patch"),
        P(None, "patch"),
        P(None, "patch"),
        P("patch", None),
        P("patch", None),
        P(None, None, "normal", "patch"),
        P(None, None, "normal", "patch"),
    )
    body = functools.partial(local, mesh.shape["patch"], mesh.shape["normal"])
    return jax.shard_map(
        body, mesh=mesh, in_specs=in_specs, out_specs=P(None, "normal", "patch"), check_vma=False
    )
```

```python
import functools

import jax
import jax.numpy as jnp
from jax import lax
from jax.experimental import pallas as pl
from jax.experimental.pallas import tpu as pltpu
from jax.sharding import PartitionSpec as P

MESH = pl.DeviceIdType.MESH
CHUNK = 8
LANES = 128
F32 = jnp.float32
BF16 = jnp.bfloat16


def halves(x):
    high = x.astype(BF16)
    return high, (x - high.astype(F32)).astype(BF16)


def dot(a, b):
    return jnp.dot(a, b, preferred_element_type=F32)


def kernel(
    patches,
    count,
    prior_hbm,
    coupling_hbm,
    slot_hbm,
    nbr_ref,
    edge_hbm,
    residual_hbm,
    upper_hbm,
    lower_hbm,
    out_ref,
    prior_ref,
    coupling_ref,
    slot_ref,
    edge_ref,
    residual,
    upper,
    lower,
    strip,
    halo,
    weight_hi,
    weight_lo,
    maps,
    force,
    up_state,
    up_out,
    up_in,
    down_out,
    down_in,
    reply_out,
    reply_in,
    last_state,
    local_sem,
    first_sem,
    strip_send,
    strip_recv,
    line_send,
    line_recv,
):
    nv, cells, lines = prior_ref.shape
    slots = coupling_ref.shape[0]
    width = edge_ref.shape[1]
    seg = cells // CHUNK
    own = lax.axis_index("patch")
    place = lax.axis_index("normal")

    first = [
        pltpu.make_async_copy(src, dst, first_sem.at[i])
        for i, (src, dst) in enumerate(
            (
                (edge_hbm, edge_ref),
                (prior_hbm, prior_ref),
                (coupling_hbm, coupling_ref),
                (slot_hbm, slot_ref),
            )
        )
    ]
    for load in first:
        load.start()
    tiles = lines // LANES
    loads = [pltpu.make_async_copy(residual_hbm, residual, local_sem.at[2, 0])]
    for i, (src, dst) in enumerate(((upper_hbm, upper), (lower_hbm, lower))):
        for t in range(tiles):
            part = src.at[:, :, :, t * LANES : (t + 1) * LANES]
            loads.append(pltpu.make_async_copy(part, dst.at[t], local_sem.at[i, t]))
    for load in loads:
        load.start()

    core = lax.rem(own, 2)
    chip = lax.rem(own // 2, 2)
    core_mate = own + 1 - 2 * core
    chip_mate = own + 2 - 4 * chip
    corner = lax.rem(chip_mate - 4 + 8 * chip + patches, patches)
    source_corner = lax.rem(own - 4 + 8 * chip + patches, patches) + 2 - 4 * chip
    direct = 3 - 3 * chip

    barrier = pltpu.get_barrier_semaphore()
    for other in (core_mate, chip_mate, source_corner):
        pl.semaphore_signal(barrier, inc=1, device_id={"patch": other}, device_id_type=MESH)

    @pl.when(place > 0)
    def _():
        pl.semaphore_signal(barrier, inc=1, device_id={"normal": place - 1}, device_id_type=MESH)

    @pl.when(place < count - 1)
    def _():
        pl.semaphore_signal(barrier, inc=1, device_id={"normal": place + 1}, device_id_type=MESH)

    for load in first:
        load.wait()
    pick = jnp.where(
        lax.broadcasted_iota(jnp.int32, (lines, width), 0) == edge_ref[...], 1.0, 0.0
    ).astype(BF16)
    prior = prior_ref[...].reshape(nv * cells, lines)
    high = prior.astype(BF16)
    rest = prior - high.astype(F32)
    middle, low = halves(rest)
    exported = dot(high, pick) + (dot(middle, pick) + dot(low, pick))
    strip[...] = exported.reshape(nv, cells, width)

    below = (place + count - 1) // count
    above = (2 * count - 2 - place) // count
    pl.semaphore_wait(barrier, 3 + below + above)

    def send(kind, v, src, slot, other):
        return pltpu.make_async_remote_copy(
            src_ref=src,
            dst_ref=halo.at[slot, v],
            send_sem=strip_send.at[kind, v],
            recv_sem=strip_recv.at[kind, v],
            device_id={"patch": other},
            device_id_type=MESH,
        )

    to_chip = [send(0, v, strip.at[v], 3 - direct, chip_mate) for v in range(nv)]
    to_core = [send(1, v, strip.at[v], 1 + core, core_mate) for v in range(nv)]
    onward = [send(2, v, strip.at[v], direct, corner) for v in range(nv)]
    across = [send(3, v, halo.at[3 - 3 * core, v], 2 - core, core_mate) for v in range(nv)]
    for copy in to_chip + onward + to_core:
        copy.start()

    row = lax.broadcasted_iota(jnp.int32, (width, lines), 0)
    offsets = (patches - 2, patches - 1, 1, 2)
    for s in range(4):
        total = jnp.zeros((width, lines), F32)
        for k in range(slots):
            relative = lax.rem(nbr_ref[0, k] - own + patches, patches)
            key = jnp.where(relative == offsets[s], slot_ref[k : k + 1, :], -1)
            total = total + jnp.where(row == key, coupling_ref[k : k + 1, :], 0.0)
        whi, wlo = halves(total)
        weight_hi[s * width : (s + 1) * width, :] = whi
        weight_lo[s * width : (s + 1) * width, :] = wlo

    def spread(ref, j, *at):
        parts = [ref[(t, *at, pl.ds(j, CHUNK, stride=seg))] for t in range(tiles)]
        return jnp.concatenate(parts, axis=1)

    def block(ref, w, v, j):
        return spread(ref, j, w, v)

    def advance(ref, j, state):
        result = []
        for v in range(nv):
            terms = [block(ref, w, v, j) * state[w] for w in range(nv)]
            result.append(((terms[0] + terms[1]) + (terms[2] + terms[3])) + terms[4])
        return result

    chunk_row = lax.broadcasted_iota(jnp.int32, (CHUNK, lines), 0)

    def shifted(x, by, reverse, fill):
        if reverse:
            return jnp.where(chunk_row < CHUNK - by, pltpu.roll(x, CHUNK - by, 0), fill)
        return jnp.where(chunk_row >= by, pltpu.roll(x, by, 0), fill)

    def map_column(ref, which, column, reverse):
        start = tuple(
            jnp.full((CHUNK, lines), 1.0 if v == column else 0.0, F32) for v in range(nv)
        )

        def one(step, state):
            j = seg - 1 - step if reverse else step
            return tuple(-x for x in advance(ref, j, state))

        end = lax.fori_loop(0, seg, one, start)
        for v in range(nv):
            maps[which, 0, v, column] = end[v]

    for load in loads:
        load.wait()
    for v in range(nv):
        map_column(upper, 0, v, False)
        map_column(lower, 1, v, True)

    def join(which, level, reverse):
        by = 1 << level
        for column in range(nv):
            prev = [
                shifted(maps[which, level, w, column], by, reverse, 1.0 if w == column else 0.0)
                for w in range(nv)
            ]
            for v in range(nv):
                total = maps[which, level, v, 0] * prev[0]
                for w in range(1, nv):
                    total = total + maps[which, level, v, w] * prev[w]
                maps[which, level + 1, v, column] = total

    for level in range(3):
        join(0, level, False)
        join(1, level, True)

    def product(which, level, v, values):
        terms = [maps[which, level, v, w] * values[w] for w in range(nv)]
        return ((terms[0] + terms[1]) + (terms[2] + terms[3])) + terms[4]

    def scanned(which, state, reverse):
        for level in range(3):
            prev = [shifted(x, 1 << level, reverse, 0.0) for x in state]
            state = [state[v] + product(which, level, v, prev) for v in range(nv)]
        return state

    def response(column):
        start = tuple(
            shifted(maps[0, 3, v, column], 1, False, 1.0 if v == column else 0.0)
            for v in range(nv)
        )

        def climb(j, state):
            state = tuple(-x for x in advance(upper, j, state))
            for v in range(nv):
                up_state[v, j] = state[v]
            return state

        def descend(step, state):
            j = seg - 1 - step
            return tuple(up_state[v, j] - x for v, x in enumerate(advance(lower, j, state)))

        lax.fori_loop(0, seg, climb, start)
        zero = tuple(jnp.zeros((CHUNK, lines), F32) for _ in range(nv))
        end = scanned(1, list(lax.fori_loop(0, seg, descend, zero)), True)
        for v in range(nv):
            reply_out[v * nv + column : v * nv + column + 1, :] = end[v][0:1, :]

    if count == 0:
        reply_out[...] = jnp.zeros_like(reply_out)
        for column in range(nv):
            response(column)
        reply = pltpu.make_async_remote_copy(
            src_ref=reply_out,
            dst_ref=reply_in,
            send_sem=line_send.at[2],
            recv_sem=line_recv.at[2],
            device_id={"normal": 1 - place},
            device_id_type=MESH,
        )

        @pl.when(place == 1)
        def _():
            reply.start()

    for v in range(nv):
        to_chip[v].wait_recv()
        onward[v].wait_recv()
        across[v].start()
    for v in range(nv):
        to_core[v].wait_recv()
        across[v].wait_recv()
    source = jnp.concatenate([halo[s].reshape(nv * cells, width) for s in range(4)], axis=1)
    source_hi, source_lo = halves(source)
    whole_hi = weight_hi[...]
    offline = dot(source_hi, whole_hi) + (dot(source_lo, whole_hi) + dot(source_hi, weight_lo[...]))
    forcing = residual[...] - offline.reshape(nv, cells, lines)
    for t in range(tiles):
        force[t] = forcing[:, :, t * LANES : (t + 1) * LANES]

    def read_force(v, j):
        return spread(force, j, v)

    def read_up(v, j):
        return up_state[v, j]

    def store_up(v, j, value):
        up_state[v, j] = value

    def store_out(v, j, value):
        for t in range(tiles):
            part = value[:, t * LANES : (t + 1) * LANES]
            force[t, v, pl.ds(j, CHUNK, stride=seg), :] = part

    def sweep(ref, which, reverse, read, store, sender, receiver, out_buf, in_buf):
        order = range(seg - 1, -1, -1) if reverse else range(seg)
        state = None
        for j in order:
            rhs = [read(v, j) for v in range(nv)]
            if state is None:
                state = rhs
            else:
                step = advance(ref, j, state)
                state = [a - b for a, b in zip(rhs, step)]
        for level in range(3):
            prev = [shifted(x, 1 << level, reverse, 0.0) for x in state]
            fresh = []
            for v in range(nv):
                terms = [maps[which, level, v, w] * prev[w] for w in range(nv)]
                fresh.append(
                    state[v] + (((terms[0] + terms[1]) + (terms[2] + terms[3])) + terms[4])
                )
            state = fresh

        has_source = place < count - 1 if reverse else place > 0
        has_target = place > 0 if reverse else place < count - 1

        @pl.when(has_source)
        def _():
            receiver.wait_recv()

        carried = [jnp.where(has_source, in_buf[v : v + 1, :], 0.0) for v in range(nv)]
        full = []
        for v in range(nv):
            terms = [maps[which, 3, v, w] * carried[w] for w in range(nv)]
            full.append(state[v] + (((terms[0] + terms[1]) + (terms[2] + terms[3])) + terms[4]))
        end = 0 if reverse else CHUNK - 1
        for v in range(nv):
            out_buf[v : v + 1, :] = full[v][end : end + 1, :]

        @pl.when(has_target)
        def _():
            sender.start()

        now = [shifted(full[v], 1, reverse, carried[v]) for v in range(nv)]
        for j in order:
            step = advance(ref, j, now)
            now = [read(v, j) - step[v] for v in range(nv)]
            for v in range(nv):
                store(v, j, now[v])

    def carry(kind, src, dst, other):
        return pltpu.make_async_remote_copy(
            src_ref=src,
            dst_ref=dst,
            send_sem=line_send.at[kind],
            recv_sem=line_recv.at[kind],
            device_id={"normal": other},
            device_id_type=MESH,
        )

    go_up = carry(0, up_out, up_in, place + 1)
    go_down = carry(1, down_out, down_in, place - 1)
    up_out[...] = jnp.zeros_like(up_out)
    down_out[...] = jnp.zeros_like(down_out)

    def partial_sweep(ref, which, reverse, read):
        state = None
        for j in range(seg - 1, -1, -1) if reverse else range(seg):
            rhs = [read(v, j) for v in range(nv)]
            if state is None:
                state = rhs
            else:
                step = advance(ref, j, state)
                state = [a - b for a, b in zip(rhs, step)]
        return scanned(which, state, reverse)

    def final_sweep(ref, reverse, read, store, now):
        for j in range(seg - 1, -1, -1) if reverse else range(seg):
            step = advance(ref, j, now)
            now = [read(v, j) - step[v] for v in range(nv)]
            for v in range(nv):
                store(v, j, now[v])

    if count == 0:
        first_up = partial_sweep(upper, 0, False, read_force)
        for v in range(nv):
            up_out[v : v + 1, :] = first_up[v][CHUNK - 1 :, :]

        @pl.when(place == 0)
        def _():
            go_up.start()

        start = [shifted(x, 1, False, 0.0) for x in first_up]
        final_sweep(upper, False, read_force, store_up, start)
        first_down = partial_sweep(lower, 1, True, read_up)
        for v in range(nv):
            down_out[v : v + 1, :] = first_down[v][0:1, :]

        @pl.when(place == 1)
        def _():
            go_down.start()
            go_up.wait_recv()
            carried = [up_in[v : v + 1, :] for v in range(nv)]
            full = [first_up[v] + product(0, 3, v, carried) for v in range(nv)]
            again = [shifted(full[v], 1, False, carried[v]) for v in range(nv)]
            final_sweep(upper, False, read_force, store_up, again)
            second_down = partial_sweep(lower, 1, True, read_up)
            for v in range(nv):
                last_state[v] = shifted(second_down[v], 1, True, 0.0)

        @pl.when(place == 0)
        def _():
            reply.wait_recv()
            go_down.wait_recv()
            carried = []
            for v in range(nv):
                total = down_in[v : v + 1, :]
                for w in range(nv):
                    at = v * nv + w
                    total = total + reply_in[at : at + 1, :] * up_out[w : w + 1, :]
                carried.append(total)
            for v in range(nv):
                full = first_down[v] + product(1, 3, v, carried)
                last_state[v] = shifted(full, 1, True, carried[v])

        final_sweep(lower, True, read_up, store_out, [last_state[v] for v in range(nv)])

        @pl.when(place == 1)
        def _():
            reply.wait_send()

    else:
        sweep(upper, 0, False, read_force, store_up, go_up, go_up, up_out, up_in)
        sweep(lower, 1, True, read_up, store_out, go_down, go_down, down_out, down_in)

    for t in range(tiles):
        out_ref[:, :, t * LANES : (t + 1) * LANES] = force[t]

    for copy in to_chip + to_core + onward + across:
        copy.wait_send()

    @pl.when(place < count - 1)
    def _():
        go_up.wait_send()

    @pl.when(place > 0)
    def _():
        go_down.wait_send()


def local(
    patches,
    count,
    residual_in,
    prior_iterate,
    coupling,
    line_slot,
    patch_nbr,
    edge_lines,
    upper_blocks,
    lower_blocks,
):
    nv, cells, lines = residual_in.shape
    width = edge_lines.shape[1]
    vmem = pl.BlockSpec(memory_space=pltpu.VMEM)
    hbm = pl.BlockSpec(memory_space=pltpu.HBM)
    seg = cells // CHUNK
    tiles = lines // LANES
    return pl.pallas_call(
        functools.partial(kernel, patches, count),
        out_shape=jax.ShapeDtypeStruct(residual_in.shape, F32),
        in_specs=[
            hbm,
            hbm,
            hbm,
            pl.BlockSpec(memory_space=pltpu.SMEM),
            hbm,
            hbm,
            hbm,
            hbm,
        ],
        out_specs=vmem,
        scratch_shapes=[
            pltpu.VMEM(prior_iterate.shape, F32),
            pltpu.VMEM(coupling.shape, F32),
            pltpu.VMEM(line_slot.shape, jnp.int32),
            pltpu.VMEM(edge_lines.shape, jnp.int32),
            pltpu.VMEM(residual_in.shape, F32),
            pltpu.VMEM((tiles, nv, nv, cells, LANES), F32),
            pltpu.VMEM((tiles, nv, nv, cells, LANES), F32),
            pltpu.VMEM((nv, cells, width), F32),
            pltpu.VMEM((4, nv, cells, width), F32),
            pltpu.VMEM((4 * width, lines), BF16),
            pltpu.VMEM((4 * width, lines), BF16),
            pltpu.VMEM((2, 4, nv, nv, CHUNK, lines), F32),
            pltpu.VMEM((tiles, nv, cells, LANES), F32),
            pltpu.VMEM((nv, seg, CHUNK, lines), F32),
            pltpu.VMEM((8, lines), F32),
            pltpu.VMEM((8, lines), F32),
            pltpu.VMEM((8, lines), F32),
            pltpu.VMEM((8, lines), F32),
            pltpu.VMEM((32, lines), F32),
            pltpu.VMEM((32, lines), F32),
            pltpu.VMEM((nv, CHUNK, lines), F32),
            pltpu.SemaphoreType.DMA((3, tiles)),
            pltpu.SemaphoreType.DMA((4,)),
            pltpu.SemaphoreType.DMA((4, nv)),
            pltpu.SemaphoreType.DMA((4, nv)),
            pltpu.SemaphoreType.DMA((3,)),
            pltpu.SemaphoreType.DMA((3,)),
        ],
        compiler_params=pltpu.CompilerParams(
            collective_id=0, has_side_effects=True, vmem_limit_bytes=60 * 2**20
        ),
    )(
        prior_iterate,
        coupling,
        line_slot,
        patch_nbr,
        edge_lines,
        residual_in,
        upper_blocks,
        lower_blocks,
    )


def solution(mesh):
    in_specs = (
        P(None, "normal", "patch"),
        P(None, "normal", "patch"),
        P(None, "patch"),
        P(None, "patch"),
        P("patch", None),
        P("patch", None),
        P(None, None, "normal", "patch"),
        P(None, None, "normal", "patch"),
    )
    body = functools.partial(local, mesh.shape["patch"], mesh.shape["normal"])
    return jax.shard_map(
        body, mesh=mesh, in_specs=in_specs, out_specs=P(None, "normal", "patch"), check_vma=False
    )
```
